512 devices in a mesh: rep: 32 (over x, z), fsdp: 16 (over y, core).
Axes of the slice: x: 4, y: 8, z: 8, core: 2. Of those that a mesh axis runs over, the one named last changes fastest.
Arguments:
- deltas: bfloat16 [32, 2, 4096, 512], P('rep', None, 'fsdp'), may hold values from -64 to 64
- weights: float32 [2, 4096, 512], P(None, 'fsdp'), may hold values from -6 to 6
- momentum: float32 [2, 4096, 512], P(None, 'fsdp'), may hold values from -0.6 to 0.6
- warm_factors: float32 [512, 2, 256], P('fsdp'), may hold values from -6 to 6
- matrix_ranks: int32 [2], replicated, may hold values from 32 to 256
Outputs:
- new_weights: float32 [2, 4096, 512], P(None, 'fsdp')
- new_momentum: float32 [2, 4096, 512], P(None, 'fsdp')
- new_factors: float32 [512, 2, 256], P('fsdp')
The draws below stay inside these ranges and needn't reach their ends.
All inputs are finite; a program needn't handle non-finite values.
Results may differ from the reference program's by a relative error of at most 0.0057.
Values may be sent and summed in bfloat16 or wider, within the bound.
A program may use at most 64 MiB of HBM per device.

```python
import math
import jax
import jax.numpy as jnp
from jax import lax

D_WIN = 4096
KVW = 512
RMAX = 256
NMAT = 2
REPLICAS = 32
N_REP = 32


def draw_deltas(key, part):
    key = jax.random.fold_in(key, 11)
    key_list = jax.random.split(key, 3)
    full_shape = (REPLICAS, NMAT, D_WIN, KVW)
    noise_part = jnp.clip(jax.random.normal(key_list[0], full_shape, jnp.float32), -4.0, 4.0)
    log_top = math.log(10.0)
    row_scale = jnp.exp(jax.random.uniform(key_list[1], (1, NMAT, D_WIN, 1), jnp.float32, 0.0, log_top))
    col_scale = jnp.exp(jax.random.uniform(key_list[2], (1, NMAT, 1, KVW), jnp.float32, 0.0, math.log(10.0)))
    return (0.1 * noise_part * row_scale * col_scale).astype(jnp.bfloat16)


def steps_of(rng, shape, shards, low, high):
    def one(dim, shards_of):
        heights = jax.random.uniform(jax.random.fold_in(jax.random.fold_in(rng, 6), dim), (shards_of,), jnp.float32, low / len(shards), high / len(shards))
        return jnp.repeat(jnp.exp(heights), shape[dim] // shards_of).reshape((-1,) + (1,) * (len(shape) - dim - 1))

    gain = one(*shards[0])
    for cut in shards[1:]:
        gain = gain * one(*cut)
    return gain


def normal_values(rng, dims, deviation, bound, cuts=(), held_as=jnp.bfloat16):
    entries = jax.random.normal(rng, dims, jnp.float32) * deviation
    if len(cuts) > 0:
        entries = steps_of(rng, dims, cuts, -0.22, 0.18) * entries
    return jnp.clip(entries, min=-bound, max=bound).astype(held_as)


def setup_inputs(seed: int = 0) -> dict:
    keys = jax.random.split(jax.random.key(seed), 6)
    return {
        "deltas": draw_deltas(jax.random.fold_in(keys[5], 71), 0),
        "weights": normal_values(keys[1], (NMAT, D_WIN, KVW), 1.0, 6.0, ((1, 16),), jnp.float32),
        "momentum": normal_values(keys[2], (NMAT, D_WIN, KVW), 0.1, 0.6, ((1, 16),), jnp.float32),
        "warm_factors": normal_values(keys[3], (KVW, NMAT, RMAX), 1.0, 6.0, ((0, 16),), jnp.float32),
        "matrix_ranks": jax.random.randint(keys[4], (NMAT,), RMAX // 8, RMAX + 1).astype(jnp.int32),
    }


OUTER_RATE = 0.7
OUTER_MOMENTUM = 0.9

def column_mask(matrix_ranks, rank_width):
    columns = jnp.arange(rank_width, dtype=jnp.int32)
    return (columns[None, :] < matrix_ranks[:, None]).astype(jnp.float32)

def reference(deltas, weights, momentum, warm_factors, matrix_ranks):
    high = lax.Precision.HIGHEST
    rank_mask = column_mask(matrix_ranks, RMAX)
    warm = warm_factors.astype(jnp.bfloat16) * rank_mask[None].astype(jnp.bfloat16)
    warm_wide = lax.optimization_barrier(warm).astype(jnp.float32)

    def left_step(summed, delta_one):
        term = jnp.einsum('mrc,cmk->mrk', delta_one.astype(jnp.float32), warm_wide, precision=high)
        return (summed + term, None)
    left_init = jnp.zeros((NMAT, D_WIN, RMAX), jnp.float32)
    left_summed, _ = lax.scan(left_step, left_init, deltas)
    left_factor = left_summed / N_REP
    filler = jnp.eye(RMAX, dtype=jnp.float32)[None] * (1.0 - rank_mask)[:, None, :]
    gram_matrix = jnp.einsum('mrk,mrj->mkj', left_factor, left_factor, precision=high) + filler
    chol_factor = jnp.linalg.cholesky(gram_matrix)
    orthonormal = lax.linalg.triangular_solve(chol_factor, left_factor, left_side=False, lower=True, transpose_a=True)
    orth_b = orthonormal.astype(jnp.bfloat16)
    orth_wide = lax.optimization_barrier(orth_b).astype(jnp.float32)

    def right_step(summed, delta_one):
        term = jnp.einsum('mrc,mrk->cmk', delta_one.astype(jnp.float32), orth_wide, precision=high)
        return (summed + term, None)
    right_init = jnp.zeros((KVW, NMAT, RMAX), jnp.float32)
    right_summed, _ = lax.scan(right_step, right_init, deltas)
    new_factors = right_summed / N_REP
    factors_b = lax.optimization_barrier(new_factors.astype(jnp.bfloat16)).astype(jnp.float32)
    approx = jnp.einsum('mrk,cmk->mrc', orth_wide, factors_b, precision=high)
    new_momentum = OUTER_MOMENTUM * momentum + approx
    new_weights = weights - OUTER_RATE * (approx + OUTER_MOMENTUM * new_momentum)
    return (new_weights, new_momentum, new_factors)
```

```python
import jax
import jax.numpy as jnp
from jax import lax
from jax.experimental import pallas as pl
from jax.experimental.pallas import tpu as pltpu
from jax.sharding import PartitionSpec as P

OUTER_RATE = 0.7
OUTER_MOMENTUM = 0.9
MESH = pl.DeviceIdType.MESH
HIGH = lax.Precision.HIGHEST
F32 = jnp.float32
BF16 = jnp.bfloat16
NX, NZ, NY = 4, 8, 8
NREP = NX * NZ
ROWS, COLS, RANK = 256, 512, 256
CH = 16
VMEM = pl.BlockSpec(memory_space=pltpu.VMEM)
REP_STEPS = [(dx, dz) for dx in range(NX) for dz in range(NZ) if (dx, dz) != (0, 0)]
NP = len(REP_STEPS)


def position():
    rep, fsdp = lax.axis_index("rep"), lax.axis_index("fsdp")
    return rep // NZ, rep % NZ, fsdp // 2, fsdp % 2


def split3(x):
    high = x.astype(BF16)
    rest = x - high.astype(F32)
    mid = rest.astype(BF16)
    low = (rest - mid.astype(F32)).astype(BF16)
    return high, mid, low


def outer_rows(a, b):
    ah, am, al = split3(a)
    bh, bm, bl = split3(b)
    left = jnp.concatenate([ah, ah, am, ah, al, am], 0)
    right = jnp.concatenate([bh, bm, bh, bl, bh, bm], 0)
    return lax.dot_general(left, right, (((0,), (0,)), ((), ())), preferred_element_type=F32)


def dot_nt(a, b, precision=HIGH):
    return lax.dot_general(a, b, (((1,), (1,)), ((), ())), precision=precision, preferred_element_type=F32)


def reduce_kernel(
    ranks_ref, deltas_ref, warm_ref,
    mfull, left_out, wfull,
    dbuf, recv_d, wtmp, mpart, recv_m, recv_y, mrow, lrow, leftbuf, send, recv, local_sem,
):
    x, z, y, c = position()
    rep = x * NZ + z
    other = 1 - c

    def at(dx, dz):
        return lax.rem(x + dx, NX) * NZ + lax.rem(z + dz, NZ)

    here = y * 2 + c
    sibling = (rep, y * 2 + other)
    columns = [(rep, lax.rem(y + d, NY) * 2 + c) for d in range(1, NY)]
    replicas = [(at(dx, dz), here) for dx, dz in REP_STEPS]

    barrier = pltpu.get_barrier_semaphore()
    for device in [sibling] + columns + replicas:
        pl.semaphore_signal(barrier, inc=1, device_id=device, device_id_type=MESH)

    lane = lax.broadcasted_iota(jnp.int32, (32, RANK), 1)
    for m in range(2):
        mask = jnp.where(lane < ranks_ref[m], 1.0, 0.0).astype(BF16)
        wtmp[m] = warm_ref[:, m, :].astype(BF16) * mask

    count = [0]
    sends = []

    def push(src, dst, device):
        k = count[0]
        count[0] += 1
        copy = pltpu.make_async_remote_copy(
            src_ref=src, dst_ref=dst, send_sem=send.at[k], recv_sem=recv.at[k],
            device_id=device, device_id_type=MESH,
        )
        copy.start()
        sends.append(copy)
        return copy

    pl.semaphore_wait(barrier, 1 + len(columns) + len(replicas))

    own = pltpu.make_async_copy(deltas_ref.at[0, c], dbuf.at[pl.ds(c * ROWS, ROWS)], local_sem)
    own.start()
    pair_d = push(deltas_ref.at[0, other], dbuf.at[pl.ds(c * ROWS, ROWS)], sibling)
    pair_w = push(wtmp.at[other], wfull.at[pl.ds(here * 32, 32)], sibling)
    wfull[pl.ds(here * 32, 32), :] = wtmp[c]
    own.wait()
    pair_d.wait_recv()
    copies_d = []
    for k, device in enumerate(replicas):
        copies_d.append(push(dbuf.at[pl.ds(device[0] * CH, CH)], recv_d.at[k], device))
    pair_w.wait_recv()
    mine = pl.ds(y * 64, 64)
    copies_w = [push(wfull.at[mine], wfull.at[mine], device) for device in columns]

    for copy in copies_d:
        copy.wait_recv()
    total = dbuf[pl.ds(rep * CH, CH), :].astype(F32)
    for k in range(NP):
        total = total + recv_d[k].astype(F32)
    mean = total * (1.0 / NREP)
    for copy in copies_w:
        copy.wait_recv()
    parts = jnp.dot(jnp.concatenate(split3(mean), 0), wfull[...], preferred_element_type=F32)
    left = parts[0:CH] + parts[CH : 2 * CH] + parts[2 * CH :]
    lrow[...] = left
    mpart[...] = outer_rows(mean, left)

    copies_m = []
    for k, device in enumerate(replicas):
        copies_m.append(push(mpart.at[pl.ds(device[0] * CH, CH)], recv_m.at[k], device))
    mine = pl.ds(rep * CH, CH)
    copies_l = [push(lrow, leftbuf.at[mine], device) for device in replicas]
    leftbuf[mine, :] = left

    for copy in copies_m:
        copy.wait_recv()
    total = mpart[mine, :]
    for k in range(NP):
        total = total + recv_m[k]
    mrow[...] = total
    copies_y = [push(mrow, recv_y.at[k], device) for k, device in enumerate(columns)]
    for copy in copies_y:
        copy.wait_recv()
    for k in range(NY - 1):
        total = total + recv_y[k]
    mfull[mine, :] = total
    copies_f = [push(mfull.at[mine], mfull.at[mine], device) for device in replicas]
    for copy in copies_l:
        copy.wait_recv()
    pair_l = push(leftbuf.at[pl.ds(other * ROWS, ROWS)], left_out.at[c], sibling)
    left_out[c] = leftbuf[pl.ds(c * ROWS, ROWS), :]
    for copy in copies_f:
        copy.wait_recv()
    pair_l.wait_recv()
    for copy in sends:
        copy.wait_send()


def reduce_all(ranks, deltas, warm):
    n = 3 + 4 * NP + 2 * (NY - 1)
    return pl.pallas_call(
        reduce_kernel,
        out_shape=(
            jax.ShapeDtypeStruct((COLS, RANK), F32),
            jax.ShapeDtypeStruct((2, ROWS, RANK), F32),
            jax.ShapeDtypeStruct((COLS, RANK), BF16),
        ),
        in_specs=[pl.BlockSpec(memory_space=pltpu.SMEM), pl.BlockSpec(memory_space=pl.ANY), VMEM],
        out_specs=(VMEM, VMEM, VMEM),
        scratch_shapes=[
            pltpu.VMEM((2 * ROWS, COLS), BF16),
            pltpu.VMEM((NP, CH, COLS), BF16),
            pltpu.VMEM((2, 32, RANK), BF16),
            pltpu.VMEM((COLS, RANK), F32),
            pltpu.VMEM((NP, CH, RANK), F32),
            pltpu.VMEM((NY - 1, CH, RANK), F32),
            pltpu.VMEM((CH, RANK), F32),
            pltpu.VMEM((CH, RANK), F32),
            pltpu.VMEM((2 * ROWS, RANK), F32),
            pltpu.SemaphoreType.DMA((n,)),
            pltpu.SemaphoreType.DMA((n,)),
            pltpu.SemaphoreType.DMA,
        ],
        compiler_params=pltpu.CompilerParams(
            collective_id=1, has_side_effects=True, vmem_limit_bytes=32 * 2**20
        ),
        name="reduce_all",
    )(ranks, deltas, warm)


def spread(x):
    return jnp.broadcast_to(x, (8, 128))


def eliminate(tiles, lane0, groups, width):
    sub = lax.broadcasted_iota(jnp.int32, (8, 128), 0)
    pivots = [None] * groups
    for b in range(groups * 8 // width):
        first = b * width // 8
        col = []
        for k in range(width):
            at = lane0 + b * width + k
            col.append([None] * first + [spread(tiles[0][g][:, at : at + 1]) for g in range(first, groups)])
        for j in range(width):
            g0, s = divmod(b * width + j, 8)
            pivot = spread(col[j][g0][s : s + 1, :])
            inverse = 1.0 / pivot
            factor = [None] * groups
            for g in range(g0, groups):
                factor[g] = jnp.where(sub > s, col[j][g], 0.0) if g == g0 else col[j][g]
            for k in range(j + 1, width):
                row = spread(col[k][g0][s : s + 1, :]) * inverse
                for g in range(g0, groups):
                    col[k][g] = col[k][g] - factor[g] * row
            for t in tiles:
                row = spread(t[g0][s : s + 1, :]) * inverse
                for g in range(g0, groups):
                    t[g] = t[g] - factor[g] * row
            pivots[g0] = pivot if s == 0 else jnp.where(sub == s, pivot, pivots[g0])
    for g in range(groups):
        scale = lax.rsqrt(pivots[g])
        for t in tiles:
            t[g] = t[g] * scale


def inverse_cholesky(a_ref):
    n, width = RANK, 32
    groups = width // 8
    for k0 in range(0, n, width):
        t0 = k0 // 128
        cols = list(range(t0, 2)) + [2 + t for t in range((k0 + width - 1) // 128 + 1)]
        rows = [slice(k0 + 8 * g, k0 + 8 * g + 8) for g in range(groups)]
        tiles = [[a_ref[r, 128 * t : 128 * t + 128] for r in rows] for t in cols]
        eliminate(tiles, k0 % 128, groups, 16)
        for i, t in enumerate(cols):
            for g, r in enumerate(rows):
                a_ref[r, 128 * t : 128 * t + 128] = tiles[i][g]
        if k0 + width < n:
            lo, hi = 128 * cols[0], 128 * cols[-1] + 128
            update = outer_rows(a_ref[k0 : k0 + width, 128 * t0 : n], a_ref[k0 : k0 + width, lo:hi])
            a_ref[k0 + width : n, lo:hi] = a_ref[k0 + width : n, lo:hi] - update[k0 + width - 128 * t0 :, :]


def factor_kernel(ranks_ref, mfull, wfull, linv, factors, factors_b, a_ref):
    core = lax.axis_index("fsdp") % 2
    rank = jnp.where(core == 0, ranks_ref[0], ranks_ref[1])
    m = mfull[...]
    three = lax.dot_general(
        wfull[...], jnp.concatenate(split3(m), 1), (((0,), (0,)), ((), ())), preferred_element_type=F32
    )
    gram = three[:, 0:RANK] + three[:, RANK : 2 * RANK] + three[:, 2 * RANK :]
    row = lax.broadcasted_iota(jnp.int32, (RANK, RANK), 0)
    column = lax.broadcasted_iota(jnp.int32, (RANK, RANK), 1)
    diagonal = row == column
    a_ref[:, 0:RANK] = gram + jnp.where(diagonal & (column >= rank), 1.0, 0.0)
    a_ref[:, RANK:] = jnp.where(diagonal, 1.0, 0.0).astype(F32)
    inverse_cholesky(a_ref)
    inverse = a_ref[:, RANK:]
    linv[...] = inverse
    new = dot_nt(m, inverse)
    factors[...] = new
    factors_b[...] = new.astype(BF16)


def factor_one(ranks, mfull, wfull):
    return pl.pallas_call(
        factor_kernel,
        out_shape=(
            jax.ShapeDtypeStruct((RANK, RANK), F32),
            jax.ShapeDtypeStruct((COLS, RANK), F32),
            jax.ShapeDtypeStruct((COLS, RANK), BF16),
        ),
        in_specs=[pl.BlockSpec(memory_space=pltpu.SMEM), VMEM, VMEM],
        out_specs=(VMEM, VMEM, VMEM),
        scratch_shapes=[pltpu.VMEM((RANK, 2 * RANK), F32)],
        compiler_params=pltpu.CompilerParams(vmem_limit_bytes=32 * 2**20),
        name="factor_one",
    )(ranks, mfull, wfull)


def swap_kernel(linv, factors, factors_b, linv_all, piece_all, factors_all, send, recv):
    rep, here = lax.axis_index("rep"), lax.axis_index("fsdp")
    core = here % 2
    other = here + 1 - 2 * core
    sibling = (rep, other)
    barrier = pltpu.get_barrier_semaphore()
    pl.semaphore_signal(barrier, inc=1, device_id=sibling, device_id_type=MESH)
    pl.semaphore_wait(barrier, 1)
    pairs = (
        (linv, linv_all.at[core]),
        (factors_b, factors_all.at[core]),
        (factors.at[pl.ds(other * 32, 32)], piece_all.at[core]),
    )
    copies = []
    for k, (src, dst) in enumerate(pairs):
        copy = pltpu.make_async_remote_copy(
            src_ref=src, dst_ref=dst, send_sem=send.at[k], recv_sem=recv.at[k],
            device_id=sibling, device_id_type=MESH,
        )
        copy.start()
        copies.append(copy)
    linv_all[core] = linv[...]
    factors_all[core] = factors_b[...]
    piece_all[core] = factors[pl.ds(here * 32, 32), :]
    for copy in copies:
        copy.wait()


def swap(linv, factors, factors_b):
    return pl.pallas_call(
        swap_kernel,
        out_shape=(
            jax.ShapeDtypeStruct((2, RANK, RANK), F32),
            jax.ShapeDtypeStruct((2, 32, RANK), F32),
            jax.ShapeDtypeStruct((2, COLS, RANK), BF16),
        ),
        in_specs=[VMEM] * 3,
        out_specs=(VMEM,) * 3,
        scratch_shapes=[pltpu.SemaphoreType.DMA((3,)), pltpu.SemaphoreType.DMA((3,))],
        compiler_params=pltpu.CompilerParams(
            collective_id=2, has_side_effects=True, vmem_limit_bytes=32 * 2**20
        ),
        name="swap",
    )(linv, factors, factors_b)


def update_kernel(left, linv, factors_b, piece, weights, momentum, new_weights, new_momentum, new_factors):
    for m in range(2):
        orth = dot_nt(left[m], linv[m]).astype(BF16)
        approx = dot_nt(orth, factors_b[m], None)
        fresh = OUTER_MOMENTUM * momentum[m] + approx
        new_momentum[m] = fresh
        new_weights[m] = weights[m] - OUTER_RATE * (approx + OUTER_MOMENTUM * fresh)
        new_factors[:, m, :] = piece[m]


def update(left, linv, factors_b, piece, weights, momentum):
    return pl.pallas_call(
        update_kernel,
        out_shape=(
            jax.ShapeDtypeStruct((2, ROWS, COLS), F32),
            jax.ShapeDtypeStruct((2, ROWS, COLS), F32),
            jax.ShapeDtypeStruct((32, 2, RANK), F32),
        ),
        in_specs=[VMEM] * 6,
        out_specs=(VMEM,) * 3,
        compiler_params=pltpu.CompilerParams(vmem_limit_bytes=32 * 2**20),
        name="update",
    )(left, linv, factors_b, piece, weights, momentum)


def shards(deltas, weights, momentum, warm_factors, matrix_ranks):
    mfull, left, wfull = reduce_all(matrix_ranks, deltas, warm_factors)
    linv, factors, factors_b = factor_one(matrix_ranks, mfull, wfull)
    linv_all, piece, factors_all = swap(linv, factors, factors_b)
    return update(left, linv_all, factors_all, piece, weights, momentum)


def solution(mesh):
    placed = (
        P("rep", None, "fsdp", None),
        P(None, "fsdp", None),
        P(None, "fsdp", None),
        P("fsdp", None, None),
        P(),
    )
    return jax.shard_map(
        shards,
        mesh=mesh,
        in_specs=placed,
        out_specs=(P(None, "fsdp", None), P(None, "fsdp", None), P("fsdp", None, None)),
        check_vma=False,
    )
```

```python
import jax
import jax.numpy as jnp
from jax import lax
from jax.experimental import pallas as pl
from jax.experimental.pallas import tpu as pltpu
from jax.sharding import PartitionSpec as P

OUTER_RATE = 0.7
OUTER_MOMENTUM = 0.9
MESH = pl.DeviceIdType.MESH
HIGH = lax.Precision.HIGHEST
F32 = jnp.float32
BF16 = jnp.bfloat16
NX, NZ, NY = 4, 8, 8
NREP = NX * NZ
ROWS, COLS, RANK = 256, 512, 256
CH = 16
HALF = RANK // 2
VMEM = pl.BlockSpec(memory_space=pltpu.VMEM)
IN_HBM = pl.BlockSpec(memory_space=pltpu.HBM)
REP_STEPS = [(dx, dz) for dx in range(NX) for dz in range(NZ) if (dx, dz) != (0, 0)]


def position():
    rep, fsdp = lax.axis_index("rep"), lax.axis_index("fsdp")
    return rep // NZ, rep % NZ, fsdp // 2, fsdp % 2


def split3(x):
    high = x.astype(BF16)
    rest = x - high.astype(F32)
    mid = rest.astype(BF16)
    low = (rest - mid.astype(F32)).astype(BF16)
    return high, mid, low


def outer_rows(a, b):
    ah, am, al = split3(a)
    bh, bm, bl = split3(b)
    left = jnp.concatenate([ah, ah, am, ah, al, am], 0)
    right = jnp.concatenate([bh, bm, bh, bl, bh, bm], 0)
    return lax.dot_general(left, right, (((0,), (0,)), ((), ())), preferred_element_type=F32)


def dot_nt(a, b, precision=HIGH):
    return lax.dot_general(a, b, (((1,), (1,)), ((), ())), precision=precision, preferred_element_type=F32)


def spread(x):
    return jnp.broadcast_to(x, (8, 128))


def eliminate(tiles, lane0, groups, width):
    sub = lax.broadcasted_iota(jnp.int32, (8, 128), 0)
    pivots = [None] * groups
    for b in range(groups * 8 // width):
        first = b * width // 8
        col = []
        for k in range(width):
            at = lane0 + b * width + k
            col.append([None] * first + [spread(tiles[0][g][:, at : at + 1]) for g in range(first, groups)])
        for j in range(width):
            g0, s = divmod(b * width + j, 8)
            pivot = spread(col[j][g0][s : s + 1, :])
            inverse = 1.0 / pivot
            factor = [None] * groups
            for g in range(g0, groups):
                factor[g] = jnp.where(sub > s, col[j][g], 0.0) if g == g0 else col[j][g]
            for k in range(j + 1, width):
                row = spread(col[k][g0][s : s + 1, :]) * inverse
                for g in range(g0, groups):
                    col[k][g] = col[k][g] - factor[g] * row
            for t in tiles:
                row = spread(t[g0][s : s + 1, :]) * inverse
                for g in range(g0, groups):
                    t[g] = t[g] - factor[g] * row
            pivots[g0] = pivot if s == 0 else jnp.where(sub == s, pivot, pivots[g0])
    for g in range(groups):
        scale = lax.rsqrt(pivots[g])
        for t in tiles:
            t[g] = t[g] * scale


def eliminate_rows(a_ref, start, stop):
    width = 32
    groups = width // 8
    for k0 in range(start, stop, width):
        t0 = k0 // 128
        cols = list(range(t0, 2)) + [2 + t for t in range((k0 + width - 1) // 128 + 1)]
        rows = [slice(k0 + 8 * g, k0 + 8 * g + 8) for g in range(groups)]
        tiles = [[a_ref[r, 128 * t : 128 * t + 128] for r in rows] for t in cols]
        eliminate(tiles, k0 % 128, groups, 16)
        for i, t in enumerate(cols):
            for g, r in enumerate(rows):
                a_ref[r, 128 * t : 128 * t + 128] = tiles[i][g]
        if k0 + width < stop:
            lo, hi = 128 * cols[0], 128 * cols[-1] + 128
            block = slice(128 * t0, 128 * t0 + 128)
            update = outer_rows(a_ref[k0 : k0 + width, block], a_ref[k0 : k0 + width, lo:hi])
            a_ref[k0 + width : stop, lo:hi] = a_ref[k0 + width : stop, lo:hi] - update[k0 + width - 128 * t0 :, :]


def three_part_tn(a, b):
    n = a.shape[1]
    out = lax.dot_general(
        jnp.concatenate(split3(a), 1), b, (((0,), (0,)), ((), ())), preferred_element_type=F32
    )
    return out[0:n] + out[n : 2 * n] + out[2 * n :]


def factor_kernel(
    ranks_hbm, deltas_hbm, warm_hbm,
    orth_all, factors_all, piece_all,
    ranks_ref, warm_ref, dbuf, recv_d, wtmp, wfull, mpart, recv_m, recv_y, mrow, mfull, lrow, leftbuf, a_ref, obuf,
    factors, local, send, sem_d, sem_m, sem_y, sem_f, sem_lz, sem_lx, sem_w, sem_p,
):
    x, z, y, c = position()
    rep = x * NZ + z
    other = 1 - c
    here = y * 2 + c
    there = y * 2 + other

    def at(dx, dz):
        return lax.rem(x + dx, NX) * NZ + lax.rem(z + dz, NZ)

    sibling = (rep, there)
    columns = [(rep, lax.rem(y + d, NY) * 2 + c) for d in range(1, NY)]
    along_z = [(at(0, dz), here) for dz in range(1, NZ)]
    along_x = [(at(dx, 0), here) for dx in range(1, NX)]
    replicas = [(at(dx, dz), here) for dx, dz in REP_STEPS]

    local_copies = [
        pltpu.make_async_copy(ranks_hbm, ranks_ref, local.at[0]),
        pltpu.make_async_copy(warm_hbm, warm_ref, local.at[1]),
        pltpu.make_async_copy(deltas_hbm.at[0, c], dbuf.at[pl.ds(c * ROWS, ROWS)], local.at[2]),
    ]
    for copy in local_copies:
        copy.start()
    barrier = pltpu.get_barrier_semaphore()
    for device in replicas + columns + [sibling]:
        pl.semaphore_signal(barrier, inc=1, device_id=device, device_id_type=MESH)

    sends = []

    def remote(src, dst, sem, device):
        return pltpu.make_async_remote_copy(
            src_ref=src, dst_ref=dst, send_sem=send.at[len(sends)], recv_sem=sem,
            device_id=device, device_id_type=MESH,
        )

    def push(src, dst, sem, device):
        copy = remote(src, dst, sem, device)
        copy.start()
        sends.append(copy)
        return copy

    for copy in local_copies:
        copy.wait()
    lane = lax.broadcasted_iota(jnp.int32, (32, RANK), 1)
    for m in range(2):
        mask = jnp.where(lane < ranks_ref[m], 1.0, 0.0).astype(BF16)
        wtmp[m] = warm_ref[:, m, :].astype(BF16) * mask
    wfull[pl.ds(here * 32, 32), :] = wtmp[c]
    pl.semaphore_wait(barrier, len(replicas) + len(columns) + 1)

    pair_d = push(deltas_hbm.at[0, other], dbuf.at[pl.ds(c * ROWS, ROWS)], sem_p.at[0], sibling)
    pair_w = push(wtmp.at[other], wfull.at[pl.ds(here * 32, 32)], sem_p.at[1], sibling)

    def push_d(x_to, dz):
        to = x_to * NZ + lax.rem(z + dz, NZ)
        slot = lax.rem(x_to - x + NX, NX) * NZ + dz
        push(dbuf.at[pl.ds(to * CH, CH)], recv_d.at[slot], sem_d.at[slot], (to, here))

    for dz in range(1, NZ):
        for step in range(2):
            push_d(2 * c + step, dz)
    pair_w.wait_recv()
    mine = pl.ds(y * 64, 64)
    copies_w = [push(wfull.at[mine], wfull.at[mine], sem_w.at[k], to) for k, to in enumerate(columns)]
    pair_d.wait_recv()
    for dz in range(1, NZ):
        for step in range(2):
            push_d(2 * other + step, dz)
    for dx in range(1, NX):
        push_d(lax.rem(x + dx, NX), 0)

    mine = pl.ds(rep * CH, CH)
    total = dbuf[mine, :].astype(F32)
    for dx, dz in REP_STEPS:
        slot = dx * NZ + dz
        remote(recv_d.at[slot], recv_d.at[slot], sem_d.at[slot], sibling).wait_recv()
        total = total + recv_d[slot].astype(F32)
    mean = total * (1.0 / NREP)
    for copy in copies_w:
        copy.wait_recv()
    parts = jnp.dot(jnp.concatenate(split3(mean), 0), wfull[...], preferred_element_type=F32)
    left = parts[0:CH] + parts[CH : 2 * CH] + parts[2 * CH :]

    copies_m = [[], []]
    for h in range(2):
        mpart[h] = outer_rows(mean, left[:, h * HALF : h * HALF + HALF])
        for k, to in enumerate(replicas):
            src = mpart.at[h, pl.ds(to[0] * CH, CH)]
            copies_m[h].append(push(src, recv_m.at[h, k], sem_m.at[h, k], to))
    lrow[...] = left
    leftbuf[mine, :] = left
    copies_lz = [push(lrow, leftbuf.at[mine], sem_lz.at[k], to) for k, to in enumerate(along_z)]

    totals = [None, None]
    copies_y = [None, None]
    for h in range(2):
        total = mpart[h, mine, :]
        for k, copy in enumerate(copies_m[h]):
            copy.wait_recv()
            total = total + recv_m[h, k]
        mrow[h] = total
        copies_y[h] = [push(mrow.at[h], recv_y.at[h, k], sem_y.at[h, k], to) for k, to in enumerate(columns)]
        totals[h] = total
    copies_f = [None, None]
    copies_lx = None
    for h in range(2):
        total = totals[h]
        for k, copy in enumerate(copies_y[h]):
            copy.wait_recv()
            total = total + recv_y[h, k]
        mfull[h, mine, :] = total
        src = mfull.at[h, mine]
        copies_f[h] = [push(src, src, sem_f.at[h, k], to) for k, to in enumerate(replicas)]
        if h == 0:
            for copy in copies_lz:
                copy.wait_recv()
            src = leftbuf.at[pl.ds(x * NZ * CH, NZ * CH)]
            copies_lx = [push(src, src, sem_lx.at[k], to) for k, to in enumerate(along_x)]

    row = lax.broadcasted_iota(jnp.int32, (HALF, RANK), 0)
    column = lax.broadcasted_iota(jnp.int32, (HALF, RANK), 1)
    rank = jnp.where(c == 0, ranks_ref[0], ranks_ref[1])
    identity = jnp.where(row == column, 1.0, 0.0).astype(F32)[:, 0:HALF]
    rest = pl.ds(HALF, HALF)

    for copy in copies_f[0]:
        copy.wait_recv()
    filler = jnp.where((row == column) & (column >= rank), 1.0, 0.0)
    a_ref[0:HALF, 0:RANK] = three_part_tn(mfull[0], wfull[...]) + filler
    a_ref[0:HALF, RANK : RANK + HALF] = identity
    eliminate_rows(a_ref, 0, HALF)
    inverse = a_ref[0:HALF, RANK : RANK + HALF]
    above = lax.dot_general(
        a_ref[0:HALF, HALF:RANK], a_ref[0:HALF, HALF : RANK + HALF],
        (((0,), (0,)), ((), ())), precision=HIGH, preferred_element_type=F32,
    )
    a_ref[HALF:RANK, RANK : RANK + HALF] = 0.0 - above[:, HALF:RANK]
    a_ref[HALF:RANK, RANK + HALF :] = identity

    pairs = []

    def finish(h, new, orth):
        cols = slice(h * HALF, h * HALF + HALF)
        factors[:, cols] = new
        factors_all[c, h] = new.astype(BF16)
        obuf[h] = orth.astype(BF16)
        orth_all[c, h] = obuf[h, pl.ds(c * ROWS, ROWS), :]
        src = factors_all.at[c, h]
        pairs.append(push(src, src, sem_p.at[2 + 2 * h], sibling))
        src = obuf.at[h, pl.ds(other * ROWS, ROWS)]
        pairs.append(push(src, orth_all.at[c, h], sem_p.at[3 + 2 * h], sibling))

    for copy in copies_lx:
        copy.wait_recv()
    finish(0, dot_nt(mfull[0], inverse), dot_nt(leftbuf[:, 0:HALF], inverse))

    for copy in copies_f[1]:
        copy.wait_recv()
    filler = jnp.where((row == column) & (column + HALF >= rank), 1.0, 0.0)[:, 0:HALF]
    a_ref[HALF:RANK, HALF:RANK] = three_part_tn(mfull[1], wfull[:, HALF:]) + filler - above[:, 0:HALF]
    eliminate_rows(a_ref, HALF, RANK)
    inverse = a_ref[HALF:RANK, RANK:]
    new = dot_nt(mfull[0], inverse[:, 0:HALF]) + dot_nt(mfull[1], inverse[:, HALF:])
    finish(1, new, dot_nt(leftbuf[...], inverse))
    pairs.append(push(factors.at[pl.ds(there * 32, 32)], piece_all.at[c], sem_p.at[6], sibling))
    piece_all[c] = factors[pl.ds(here * 32, 32), :]
    for copy in pairs:
        copy.wait_recv()
    for copy in sends:
        copy.wait_send()


def factor_all(ranks, deltas, warm):
    others = len(REP_STEPS)
    total = 2 + others + (NY - 1) + 2 * others + (NZ - 1) + 2 * (NY - 1) + 2 * others + (NX - 1) + 5
    dma = pltpu.SemaphoreType.DMA
    return pl.pallas_call(
        factor_kernel,
        out_shape=(
            jax.ShapeDtypeStruct((2, 2, ROWS, HALF), BF16),
            jax.ShapeDtypeStruct((2, 2, COLS, HALF), BF16),
            jax.ShapeDtypeStruct((2, 32, RANK), F32),
        ),
        in_specs=[IN_HBM] * 3,
        out_specs=(VMEM,) * 3,
        scratch_shapes=[
            pltpu.SMEM((2,), jnp.int32),
            pltpu.VMEM((32, 2, RANK), F32),
            pltpu.VMEM((2 * ROWS, COLS), BF16),
            pltpu.VMEM((NREP, CH, COLS), BF16),
            pltpu.VMEM((2, 32, RANK), BF16),
            pltpu.VMEM((COLS, RANK), BF16),
            pltpu.VMEM((2, COLS, HALF), F32),
            pltpu.VMEM((2, others, CH, HALF), F32),
            pltpu.VMEM((2, NY - 1, CH, HALF), F32),
            pltpu.VMEM((2, CH, HALF), F32),
            pltpu.VMEM((2, COLS, HALF), F32),
            pltpu.VMEM((CH, RANK), F32),
            pltpu.VMEM((2 * ROWS, RANK), F32),
            pltpu.VMEM((RANK, 2 * RANK), F32),
            pltpu.VMEM((2, 2 * ROWS, HALF), BF16),
            pltpu.VMEM((COLS, RANK), F32),
            dma((3,)), dma((total,)), dma((NREP,)), dma((2, others)), dma((2, NY - 1)), dma((2, others)),
            dma((NZ - 1,)), dma((NX - 1,)), dma((NY - 1,)), dma((7,)),
        ],
        compiler_params=pltpu.CompilerParams(
            collective_id=1, has_side_effects=True, vmem_limit_bytes=32 * 2**20
        ),
        name="factor_all",
        cost_estimate=pl.CostEstimate(flops=10**9, bytes_accessed=0, transcendentals=0),
    )(*(pltpu.with_memory_space_constraint(a, pltpu.HBM) for a in (ranks, deltas, warm)))


def update_kernel(orth, factors, piece, weights, momentum, new_weights, new_momentum, new_factors):
    for m in range(2):
        approx = dot_nt(orth[m, 0], factors[m, 0], None) + dot_nt(orth[m, 1], factors[m, 1], None)
        fresh = OUTER_MOMENTUM * momentum[m] + approx
        new_momentum[m] = fresh
        new_weights[m] = weights[m] - OUTER_RATE * (approx + OUTER_MOMENTUM * fresh)
        new_factors[:, m, :] = piece[m]


def update(orth, factors, piece, weights, momentum):
    return pl.pallas_call(
        update_kernel,
        out_shape=(
            jax.ShapeDtypeStruct((2, ROWS, COLS), F32),
            jax.ShapeDtypeStruct((2, ROWS, COLS), F32),
            jax.ShapeDtypeStruct((32, 2, RANK), F32),
        ),
        in_specs=[VMEM] * 5,
        out_specs=(VMEM,) * 3,
        compiler_params=pltpu.CompilerParams(vmem_limit_bytes=32 * 2**20),
        name="update",
    )(orth, factors, piece, weights, momentum)


def shards(deltas, weights, momentum, warm_factors, matrix_ranks):
    orth, factors, piece = factor_all(matrix_ranks, deltas, warm_factors)
    return update(orth, factors, piece, weights, momentum)


def solution(mesh):
    placed = (
        P("rep", None, "fsdp", None),
        P(None, "fsdp", None),
        P(None, "fsdp", None),
        P("fsdp", None, None),
        P(),
    )
    return jax.shard_map(
        shards,
        mesh=mesh,
        in_specs=placed,
        out_specs=(P(None, "fsdp", None), P(None, "fsdp", None), P("fsdp", None, None)),
        check_vma=False,
    )
```

```python
import jax
import jax.numpy as jnp
from jax import lax
from jax.experimental import pallas as pl
from jax.experimental.pallas import tpu as pltpu
from jax.sharding import PartitionSpec as P

OUTER_RATE = 0.7
OUTER_MOMENTUM = 0.9
MESH = pl.DeviceIdType.MESH
F32 = jnp.float32
BF16 = jnp.bfloat16
NX, NZ, NY = 4, 8, 8
NREP = NX * NZ
ROWS, COLS, RANK = 256, 512, 256
CH = 16
UNIT = 64
UNITS = RANK // UNIT
PIECES = ((0, 128), (128, 256))
PLANES = "zy"
SCHEDULE = "mmyy"
WIDE = COLS + 2 * ROWS
VMEM = pl.BlockSpec(memory_space=pltpu.VMEM)
IN_HBM = pl.BlockSpec(memory_space=pltpu.HBM)
PLANE_STEPS = [(dx, d) for dx in range(NX) for d in range(NY) if dx and d]
REP_STEPS = [(dx, dz) for dx in range(NX) for dz in range(NZ) if (dx, dz) != (0, 0)]


def position():
    rep, fsdp = lax.axis_index("rep"), lax.axis_index("fsdp")
    return rep // NZ, rep % NZ, fsdp // 2, fsdp % 2


def split3(x):
    high = x.astype(BF16)
    rest = x - high.astype(F32)
    mid = rest.astype(BF16)
    low = (rest - mid.astype(F32)).astype(BF16)
    return high, mid, low


def outer_rows(a, b):
    ah, am, al = split3(a)
    bh, bm, bl = split3(b)
    left = jnp.concatenate([ah, ah, am, ah, al, am], 0)
    right = jnp.concatenate([bh, bm, bh, bl, bh, bm], 0)
    return lax.dot_general(left, right, (((0,), (0,)), ((), ())), preferred_element_type=F32)


def six_lanes(a):
    high, mid, low = split3(a)
    return jnp.concatenate([high, high, mid, high, low, mid], 1)


def six_rows(parts):
    high, mid, low = parts
    return jnp.concatenate([high, mid, high, low, high, mid], 0)


def spread(x):
    return jnp.broadcast_to(x, (8, 128))


def eliminate(tiles, lane0, groups, width):
    sub = lax.broadcasted_iota(jnp.int32, (8, 128), 0)
    pivots = [None] * groups
    for b in range(groups * 8 // width):
        first = b * width // 8
        col = []
        for k in range(width):
            at = lane0 + b * width + k
            col.append([None] * first + [spread(tiles[0][g][:, at : at + 1]) for g in range(first, groups)])
        for j in range(width):
            g0, s = divmod(b * width + j, 8)
            pivot = spread(col[j][g0][s : s + 1, :])
            inverse = 1.0 / pivot
            factor = [None] * groups
            for g in range(g0, groups):
                factor[g] = jnp.where(sub > s, col[j][g], 0.0) if g == g0 else col[j][g]
            for k in range(j + 1, width):
                row = spread(col[k][g0][s : s + 1, :]) * inverse
                for g in range(g0, groups):
                    col[k][g] = col[k][g] - factor[g] * row
            for t in tiles:
                row = spread(t[g0][s : s + 1, :]) * inverse
                for g in range(g0, groups):
                    t[g] = t[g] - factor[g] * row
            pivots[g0] = pivot if s == 0 else jnp.where(sub == s, pivot, pivots[g0])
    for g in range(groups):
        scale = lax.rsqrt(pivots[g])
        for t in tiles:
            t[g] = t[g] * scale


def eliminate_rows(a_ref, start, stop):
    width = 32
    groups = width // 8
    for k0 in range(start, stop, width):
        t0 = k0 // 128
        cols = list(range(t0, RANK // 128)) + [RANK // 128]
        rows = [slice(k0 + 8 * g, k0 + 8 * g + 8) for g in range(groups)]
        tiles = [[a_ref[r, 128 * t : 128 * t + 128] for r in rows] for t in cols]
        eliminate(tiles, k0 % 128, groups, 16)
        for i, t in enumerate(cols):
            for g, r in enumerate(rows):
                a_ref[r, 128 * t : 128 * t + 128] = tiles[i][g]
        if k0 + width < stop:
            block = slice(128 * t0, 128 * t0 + 128)
            update = outer_rows(a_ref[k0 : k0 + width, block], a_ref[k0 : k0 + width, 128 * t0 :])
            rest = slice(k0 + width - 128 * t0, stop - 128 * t0)
            a_ref[k0 + width : stop, 128 * t0 :] = a_ref[k0 + width : stop, 128 * t0 :] - update[rest, :]


def factor_kernel(
    ranks_hbm, deltas_hbm, warm_hbm,
    orth_all, factors_all, piece_all,
    ranks_ref, warm_ref, dbuf, recv_d, wtmp, wfull, mpart, recv_m, recv_y, mrow, mfull, lrow, leftbuf, left_t, a_ref,
    solved, obuf, blocks, local, send, sem_d, sem_m, sem_y, sem_f, sem_lz, sem_lx, sem_w, sem_p,
):
    x, z, y, c = position()
    rep = x * NZ + z
    other = 1 - c
    here = y * 2 + c
    there = y * 2 + other

    def at(dx, dz):
        return lax.rem(x + dx, NX) * NZ + lax.rem(z + dz, NZ)

    sibling = (rep, there)
    columns = [(rep, lax.rem(y + d, NY) * 2 + c) for d in range(1, NY)]
    along_z = [(at(0, dz), here) for dz in range(1, NZ)]
    along_x = [(at(dx, 0), here) for dx in range(1, NX)]
    replicas = [(at(dx, dz), here) for dx, dz in REP_STEPS]

    def across(dx, dy):
        return lax.rem(x + dx, NX), lax.rem(y + dy, NY)

    in_xy = [across(dx, dy) for dx, dy in REP_STEPS]
    in_xy = [((to_x * NZ + z, to_y * 2 + c), to_x * NY + to_y) for to_x, to_y in in_xy]
    in_xz = [(device, device[0]) for device in replicas]
    planes = [in_xz if plane == "z" else in_xy for plane in PLANES]
    owned = [rep if plane == "z" else x * NY + y for plane in PLANES]
    lines = [columns if plane == "z" else along_z for plane in PLANES]
    corners = [in_xy[k][0] for k, step in enumerate(REP_STEPS) if step in PLANE_STEPS]

    local_copies = [
        pltpu.make_async_copy(ranks_hbm, ranks_ref, local.at[0]),
        pltpu.make_async_copy(warm_hbm, warm_ref, local.at[1]),
        pltpu.make_async_copy(deltas_hbm.at[0, c], dbuf.at[pl.ds(c * ROWS, ROWS)], local.at[2]),
    ]
    for copy in local_copies:
        copy.start()
    barrier = pltpu.get_barrier_semaphore()
    for device in replicas + columns + corners + [sibling]:
        pl.semaphore_signal(barrier, inc=1, device_id=device, device_id_type=MESH)

    sends = []

    def remote(src, dst, sem, device):
        return pltpu.make_async_remote_copy(
            src_ref=src, dst_ref=dst, send_sem=send.at[len(sends)], recv_sem=sem,
            device_id=device, device_id_type=MESH,
        )

    def push(src, dst, sem, device):
        copy = remote(src, dst, sem, device)
        copy.start()
        sends.append(copy)
        return copy

    for copy in local_copies:
        copy.wait()
    lane = lax.broadcasted_iota(jnp.int32, (32, RANK), 1)
    for m in range(2):
        mask = jnp.where(lane < ranks_ref[m], 1.0, 0.0).astype(BF16)
        wtmp[m] = warm_ref[:, m, :].astype(BF16) * mask
    wfull[pl.ds(here * 32, 32), :] = wtmp[c]
    pl.semaphore_wait(barrier, len(replicas) + len(columns) + len(corners) + 1)

    pair_d = push(deltas_hbm.at[0, other], dbuf.at[pl.ds(c * ROWS, ROWS)], sem_p.at[0], sibling)
    pair_w = push(wtmp.at[other], wfull.at[pl.ds(here * 32, 32)], sem_p.at[1], sibling)

    def push_d(x_to, dz):
        to = x_to * NZ + lax.rem(z + dz, NZ)
        slot = lax.rem(x_to - x + NX, NX) * NZ + dz
        push(dbuf.at[pl.ds(to * CH, CH)], recv_d.at[slot], sem_d.at[slot], (to, here))

    for dz in range(1, NZ):
        for step in range(2):
            push_d(2 * c + step, dz)
    pair_w.wait_recv()
    mine = pl.ds(y * 64, 64)
    copies_w = [push(wfull.at[mine], wfull.at[mine], sem_w.at[k], to) for k, to in enumerate(columns)]
    pair_d.wait_recv()
    for dz in range(1, NZ):
        for step in range(2):
            push_d(2 * other + step, dz)
    for dx in range(1, NX):
        push_d(lax.rem(x + dx, NX), 0)

    mine = pl.ds(rep * CH, CH)
    total = dbuf[mine, :].astype(F32)
    for dx, dz in REP_STEPS:
        slot = dx * NZ + dz
        remote(recv_d.at[slot], recv_d.at[slot], sem_d.at[slot], sibling).wait_recv()
        total = total + recv_d[slot].astype(F32)
    mean = total * (1.0 / NREP)
    for copy in copies_w:
        copy.wait_recv()
    parts = jnp.dot(jnp.concatenate(split3(mean), 0), wfull[...], preferred_element_type=F32)
    left = parts[0:CH] + parts[CH : 2 * CH] + parts[2 * CH :]

    for h in range(RANK // 128):
        product = outer_rows(left[:, 128 * h : 128 * h + 128], mean)
        for u in range(128 // UNIT):
            for r in range(NREP):
                i, j = UNIT * u + 8 * (r // 4), 128 * (r % 4)
                mpart[h * (128 // UNIT) + u, r] = product[i : i + 8, j : j + 128]
    lrow[...] = left
    leftbuf[mine, :] = left
    units = [pl.ds(start // UNIT, (stop - start) // UNIT) for start, stop in PIECES]
    copies_m = []
    for p, unit in enumerate(units):
        copies_m.append(
            [
                push(mpart.at[unit, chunk], recv_m.at[k, unit], sem_m.at[p, k], to)
                for k, (to, chunk) in enumerate(planes[p])
            ]
        )
    copies_lz = [push(lrow, leftbuf.at[mine], sem_lz.at[k], to) for k, to in enumerate(along_z)]

    copies_y, copies_f = [], []
    copies_lx = None
    for event in SCHEDULE:
        if event == "m":
            p = len(copies_y)
            for copy in copies_m[p]:
                copy.wait_recv()
            total = mpart[units[p], owned[p]]
            for k in range(len(replicas)):
                total = total + recv_m[k, units[p]]
            mrow[units[p]] = total
            copies_y.append(
                [push(mrow.at[units[p]], recv_y.at[k, units[p]], sem_y.at[p, k], to) for k, to in enumerate(lines[p])]
            )
        else:
            p = len(copies_f)
            for copy in copies_y[p]:
                copy.wait_recv()
            total = mrow[units[p]]
            for k in range(NY - 1):
                total = total + recv_y[k, units[p]]
            mfull[units[p], owned[p]] = total
            src = mfull.at[units[p], owned[p]]
            copies_f.append([push(src, src, sem_f.at[p, k], to) for k, (to, _) in enumerate(planes[p])])
            if p == 0:
                for copy in copies_lz:
                    copy.wait_recv()
                src = leftbuf.at[pl.ds(x * NZ * CH, NZ * CH)]
                copies_lx = [push(src, src, sem_lx.at[k], to) for k, to in enumerate(along_x)]
    waited = len(sends) - 2 * len(replicas)
    for copy in sends[:waited]:
        copy.wait_send()
    rank = jnp.where(c == 0, ranks_ref[0], ranks_ref[1])
    pairs = []
    for p, (start, stop) in enumerate(PIECES):
        n = stop - start
        block = start // 128 * 128
        less = None
        if p > 0:
            parts = [solved[i, 0:start, :] for i in range(3)]
            above = split3(a_ref[0:start, block : block + 128])
            above = jnp.concatenate([above[0], above[0], above[1], above[0], above[2], above[1]], 0)
            less = lax.dot_general(
                above, six_rows(parts), (((0,), (0,)), ((), ())), preferred_element_type=F32
            )[start - block : stop - block, :]
        for copy in copies_f[p]:
            copy.wait_recv()
        rows = []
        for u in range(start // UNIT, stop // UNIT):
            for g in range(8):
                rows.append(jnp.concatenate([mfull[u, 4 * g + t] for t in range(4)], 1))
        wide = jnp.concatenate(rows, 0)
        if p > 0:
            wide = wide - less[:, 0:COLS]
        parts = split3(wide)
        three = jnp.dot(jnp.concatenate(parts, 0), wfull[...], preferred_element_type=F32)
        row = lax.broadcasted_iota(jnp.int32, (n, RANK), 0)
        column = lax.broadcasted_iota(jnp.int32, (n, RANK), 1)
        filler = jnp.where((row + start == column) & (column >= rank), 1.0, 0.0)
        a_ref[start:stop, 0:RANK] = three[0:n] + three[n : 2 * n] + three[2 * n :] + filler
        a_ref[start:stop, RANK:] = jnp.where(row == column, 1.0, 0.0).astype(F32)[:, 0:128]
        eliminate_rows(a_ref, start, stop)
        inverse = six_lanes(a_ref[start:stop, RANK : RANK + n])
        mine = pl.ds(start, n)

        rows = jnp.dot(inverse, six_rows(parts), preferred_element_type=F32)
        last = stop == RANK
        factors_all[c, mine, :] = rows.astype(BF16)
        if not last:
            for i, part in enumerate(split3(rows)):
                solved[i, start:stop, 0:COLS] = part
        for t in range(4):
            blocks[t, mine, :] = rows[:, 128 * t : 128 * t + 128]
        src = factors_all.at[c, mine]
        pairs.append(push(src, src, sem_p.at[2 + 3 * p], sibling))
        pairs.append(push(blocks.at[y // 2, mine], piece_all.at[c, mine], sem_p.at[4 + 3 * p], sibling))
        piece_all[c, mine, :] = blocks[y // 2, mine, :]

        if p == 0:
            for copy in copies_lx:
                copy.wait_recv()
            for g in range(4):
                left_t[:, 128 * g : 128 * g + 128] = jnp.transpose(leftbuf[128 * g : 128 * g + 128, :])
        wide = left_t[start:stop, :]
        if p > 0:
            wide = wide - less[:, COLS:]
        rows = jnp.dot(inverse, six_rows(split3(wide)), preferred_element_type=F32)
        if not last:
            for i, part in enumerate(split3(rows)):
                solved[i, start:stop, COLS:] = part
        low_rows, high_rows = rows[:, 0:ROWS].astype(BF16), rows[:, ROWS:].astype(BF16)
        own_side = jnp.broadcast_to(c, (n, ROWS)) == 0
        obuf[mine, :] = jnp.where(own_side, high_rows, low_rows)
        pairs.append(push(obuf.at[mine], orth_all.at[c, mine], sem_p.at[3 + 3 * p], sibling))
        orth_all[c, mine, :] = jnp.where(own_side, low_rows, high_rows)
    for copy in pairs:
        copy.wait_recv()
    for copy in sends[waited:]:
        copy.wait_send()


def factor_all(ranks, deltas, warm):
    others, pieces = len(REP_STEPS), len(PIECES)
    total = 2 + others + (NY - 1) + pieces * (2 * others + NY - 1 + 3) + (NZ - 1) + (NX - 1)
    dma = pltpu.SemaphoreType.DMA
    return pl.pallas_call(
        factor_kernel,
        out_shape=(
            jax.ShapeDtypeStruct((2, RANK, ROWS), BF16),
            jax.ShapeDtypeStruct((2, RANK, COLS), BF16),
            jax.ShapeDtypeStruct((2, RANK, 128), F32),
        ),
        in_specs=[IN_HBM] * 3,
        out_specs=(VMEM,) * 3,
        scratch_shapes=[
            pltpu.SMEM((2,), jnp.int32),
            pltpu.VMEM((32, 2, RANK), F32),
            pltpu.VMEM((2 * ROWS, COLS), BF16),
            pltpu.VMEM((NREP, CH, COLS), BF16),
            pltpu.VMEM((2, 32, RANK), BF16),
            pltpu.VMEM((COLS, RANK), BF16),
            pltpu.VMEM((UNITS, NREP, 8, 128), F32),
            pltpu.VMEM((others, UNITS, 8, 128), F32),
            pltpu.VMEM((NY - 1, UNITS, 8, 128), F32),
            pltpu.VMEM((UNITS, 8, 128), F32),
            pltpu.VMEM((UNITS, NREP, 8, 128), F32),
            pltpu.VMEM((CH, RANK), F32),
            pltpu.VMEM((2 * ROWS, RANK), F32),
            pltpu.VMEM((RANK, 2 * ROWS), F32),
            pltpu.VMEM((RANK, RANK + 128), F32),
            pltpu.VMEM((3, RANK, WIDE), BF16),
            pltpu.VMEM((RANK, ROWS), BF16),
            pltpu.VMEM((4, RANK, 128), F32),
            dma((3,)), dma((total,)), dma((NREP,)), dma((pieces, others)), dma((pieces, NY - 1)),
            dma((pieces, others)), dma((NZ - 1,)), dma((NX - 1,)), dma((NY - 1,)), dma((2 + 3 * pieces,)),
        ],
        compiler_params=pltpu.CompilerParams(
            collective_id=1, has_side_effects=True, vmem_limit_bytes=32 * 2**20
        ),
        name="factor_all",
        cost_estimate=pl.CostEstimate(flops=10**9, bytes_accessed=0, transcendentals=0),
    )(*(pltpu.with_memory_space_constraint(a, pltpu.HBM) for a in (ranks, deltas, warm)))


def update_kernel(orth, factors, piece, weights, momentum, new_weights, new_momentum, new_factors, turned):
    offset = lax.axis_index("fsdp") % 4 * 32
    for m in range(2):
        approx = lax.dot_general(orth[m], factors[m], (((0,), (0,)), ((), ())), preferred_element_type=F32)
        fresh = OUTER_MOMENTUM * momentum[m] + approx
        new_momentum[m] = fresh
        new_weights[m] = weights[m] - OUTER_RATE * (approx + OUTER_MOMENTUM * fresh)
        turned[m] = jnp.transpose(piece[m])
        new_factors[:, m, :] = turned[m, pl.ds(offset, 32), :]


def update(orth, factors, piece, weights, momentum):
    return pl.pallas_call(
        update_kernel,
        out_shape=(
            jax.ShapeDtypeStruct((2, ROWS, COLS), F32),
            jax.ShapeDtypeStruct((2, ROWS, COLS), F32),
            jax.ShapeDtypeStruct((32, 2, RANK), F32),
        ),
        in_specs=[VMEM] * 5,
        out_specs=(VMEM,) * 3,
        scratch_shapes=[pltpu.VMEM((2, 128, RANK), F32)],
        compiler_params=pltpu.CompilerParams(vmem_limit_bytes=32 * 2**20),
        name="update",
    )(orth, factors, piece, weights, momentum)


def shards(deltas, weights, momentum, warm_factors, matrix_ranks):
    orth, factors, piece = factor_all(matrix_ranks, deltas, warm_factors)
    return update(orth, factors, piece, weights, momentum)


def solution(mesh):
    placed = (
        P("rep", None, "fsdp", None),
        P(None, "fsdp", None),
        P(None, "fsdp", None),
        P("fsdp", None, None),
        P(),
    )
    return jax.shard_map(
        shards,
        mesh=mesh,
        in_specs=placed,
        out_specs=(P(None, "fsdp", None), P(None, "fsdp", None), P("fsdp", None, None)),
        check_vma=False,
    )
```

```python
import jax
import jax.numpy as jnp
from jax import lax
from jax.experimental import pallas as pl
from jax.experimental.pallas import tpu as pltpu
from jax.sharding import PartitionSpec as P

OUTER_RATE = 0.7
OUTER_MOMENTUM = 0.9
MESH = pl.DeviceIdType.MESH
F32 = jnp.float32
BF16 = jnp.bfloat16
NX, NZ, NY = 4, 8, 8
NREP = NX * NZ
ROWS, COLS, RANK = 256, 512, 256
CH = 16
UNIT = 64
UNITS = RANK // UNIT
PIECES = ((0, 128), (128, 256))
PLANES = "zy"
SCHEDULE = "mmlyy"
WIDE = COLS + 2 * ROWS
VMEM = pl.BlockSpec(memory_space=pltpu.VMEM)
IN_HBM = pl.BlockSpec(memory_space=pltpu.HBM)
PLANE_STEPS = [(dx, d) for dx in range(NX) for d in range(NY) if dx and d]
REP_STEPS = [(dx, dz) for dx in range(NX) for dz in range(NZ) if (dx, dz) != (0, 0)]


def position():
    rep, fsdp = lax.axis_index("rep"), lax.axis_index("fsdp")
    return rep // NZ, rep % NZ, fsdp // 2, fsdp % 2


def split3(x):
    high = x.astype(BF16)
    rest = x - high.astype(F32)
    mid = rest.astype(BF16)
    low = (rest - mid.astype(F32)).astype(BF16)
    return high, mid, low


def outer_rows(a, b):
    ah, am, al = split3(a)
    bh, bm, bl = split3(b)
    left = jnp.concatenate([ah, ah, am, ah, al, am], 0)
    right = jnp.concatenate([bh, bm, bh, bl, bh, bm], 0)
    return lax.dot_general(left, right, (((0,), (0,)), ((), ())), preferred_element_type=F32)


def six_lanes(a):
    high, mid, low = split3(a)
    return jnp.concatenate([high, high, mid, high, low, mid], 1)


def six_rows(parts):
    high, mid, low = parts
    return jnp.concatenate([high, mid, high, low, high, mid], 0)


def spread(x):
    return jnp.broadcast_to(x, (8, 128))


def eliminate(tiles, lane0, groups, width):
    sub = lax.broadcasted_iota(jnp.int32, (8, 128), 0)
    pivots = [None] * groups
    for b in range(groups * 8 // width):
        first = b * width // 8
        col = []
        for k in range(width):
            at = lane0 + b * width + k
            col.append([None] * first + [spread(tiles[0][g][:, at : at + 1]) for g in range(first, groups)])
        for j in range(width):
            g0, s = divmod(b * width + j, 8)
            pivot = spread(col[j][g0][s : s + 1, :])
            inverse = 1.0 / pivot
            factor = [None] * groups
            for g in range(g0, groups):
                factor[g] = jnp.where(sub > s, col[j][g], 0.0) if g == g0 else col[j][g]
            for k in range(j + 1, width):
                row = spread(col[k][g0][s : s + 1, :]) * inverse
                for g in range(g0, groups):
                    col[k][g] = col[k][g] - factor[g] * row
            for t in tiles:
                row = spread(t[g0][s : s + 1, :]) * inverse
                for g in range(g0, groups):
                    t[g] = t[g] - factor[g] * row
            pivots[g0] = pivot if s == 0 else jnp.where(sub == s, pivot, pivots[g0])
    for g in range(groups):
        scale = lax.rsqrt(pivots[g])
        for t in tiles:
            t[g] = t[g] * scale


def eliminate_rows(a_ref, start, stop):
    width = 32
    groups = width // 8
    for k0 in range(start, stop, width):
        t0 = k0 // 128
        cols = list(range(t0, RANK // 128)) + [RANK // 128]
        rows = [slice(k0 + 8 * g, k0 + 8 * g + 8) for g in range(groups)]
        tiles = [[a_ref[r, 128 * t : 128 * t + 128] for r in rows] for t in cols]
        eliminate(tiles, k0 % 128, groups, 16)
        for i, t in enumerate(cols):
            for g, r in enumerate(rows):
                a_ref[r, 128 * t : 128 * t + 128] = tiles[i][g]
        if k0 + width < stop:
            block = slice(128 * t0, 128 * t0 + 128)
            update = outer_rows(a_ref[k0 : k0 + width, block], a_ref[k0 : k0 + width, 128 * t0 :])
            rest = slice(k0 + width - 128 * t0, stop - 128 * t0)
            a_ref[k0 + width : stop, 128 * t0 :] = a_ref[k0 + width : stop, 128 * t0 :] - update[rest, :]


def factor_kernel(
    ranks_hbm, deltas_hbm, warm_hbm,
    orth_all, factors_all, piece_all,
    ranks_ref, warm_ref, dbuf, recv_d, wtmp, wfull, mpart, recv_m, recv_y, mrow, mfull, lrow, leftbuf, left_t, a_ref,
    solved, obuf, blocks, local, send, sem_d, sem_m, sem_y, sem_f, sem_lz, sem_lx, sem_w, sem_p,
):
    x, z, y, c = position()
    rep = x * NZ + z
    other = 1 - c
    here = y * 2 + c
    there = y * 2 + other

    def at(dx, dz):
        return lax.rem(x + dx, NX) * NZ + lax.rem(z + dz, NZ)

    sibling = (rep, there)
    columns = [(rep, lax.rem(y + d, NY) * 2 + c) for d in range(1, NY)]
    along_z = [(at(0, dz), here) for dz in range(1, NZ)]
    along_x = [(at(dx, 0), here) for dx in range(1, NX)]
    replicas = [(at(dx, dz), here) for dx, dz in REP_STEPS]

    def across(dx, dy):
        return lax.rem(x + dx, NX), lax.rem(y + dy, NY)

    in_xy = [across(dx, dy) for dx, dy in REP_STEPS]
    in_xy = [((to_x * NZ + z, to_y * 2 + c), to_x * NY + to_y) for to_x, to_y in in_xy]
    in_xz = [(device, device[0]) for device in replicas]
    planes = [in_xz if plane == "z" else in_xy for plane in PLANES]
    owned = [rep if plane == "z" else x * NY + y for plane in PLANES]
    lines = [columns if plane == "z" else along_z for plane in PLANES]
    corners = [in_xy[k][0] for k, step in enumerate(REP_STEPS) if step in PLANE_STEPS]

    local_copies = [
        pltpu.make_async_copy(ranks_hbm, ranks_ref, local.at[0]),
        pltpu.make_async_copy(warm_hbm, warm_ref, local.at[1]),
        pltpu.make_async_copy(deltas_hbm.at[0, c], dbuf.at[pl.ds(c * ROWS, ROWS)], local.at[2]),
    ]
    for copy in local_copies:
        copy.start()
    barrier = pltpu.get_barrier_semaphore()
    for device in replicas + columns + corners + [sibling]:
        pl.semaphore_signal(barrier, inc=1, device_id=device, device_id_type=MESH)

    sends = []

    def remote(src, dst, sem, device):
        return pltpu.make_async_remote_copy(
            src_ref=src, dst_ref=dst, send_sem=send.at[len(sends)], recv_sem=sem,
            device_id=device, device_id_type=MESH,
        )

    def push(src, dst, sem, device):
        copy = remote(src, dst, sem, device)
        copy.start()
        sends.append(copy)
        return copy

    for copy in local_copies:
        copy.wait()
    lane = lax.broadcasted_iota(jnp.int32, (32, RANK), 1)
    for m in range(2):
        mask = jnp.where(lane < ranks_ref[m], 1.0, 0.0).astype(BF16)
        wtmp[m] = warm_ref[:, m, :].astype(BF16) * mask
    wfull[pl.ds(here * 32, 32), :] = wtmp[c]
    pl.semaphore_wait(barrier, len(replicas) + len(columns) + len(corners) + 1)

    pair_d = push(deltas_hbm.at[0, other], dbuf.at[pl.ds(c * ROWS, ROWS)], sem_p.at[0], sibling)
    pair_w = push(wtmp.at[other], wfull.at[pl.ds(here * 32, 32)], sem_p.at[1], sibling)

    def push_d(x_to, dz):
        to = x_to * NZ + lax.rem(z + dz, NZ)
        slot = lax.rem(x_to - x + NX, NX) * NZ + dz
        push(dbuf.at[pl.ds(to * CH, CH)], recv_d.at[slot], sem_d.at[slot], (to, here))

    for dz in range(1, NZ):
        for step in range(2):
            push_d(2 * c + step, dz)
    pair_w.wait_recv()
    mine = pl.ds(y * 64, 64)
    copies_w = [push(wfull.at[mine], wfull.at[mine], sem_w.at[k], to) for k, to in enumerate(columns)]
    pair_d.wait_recv()
    for dz in range(1, NZ):
        for step in range(2):
            push_d(2 * other + step, dz)
    for dx in range(1, NX):
        push_d(lax.rem(x + dx, NX), 0)

    mine = pl.ds(rep * CH, CH)
    total = dbuf[mine, :].astype(F32)
    for dx, dz in REP_STEPS:
        slot = dx * NZ + dz
        remote(recv_d.at[slot], recv_d.at[slot], sem_d.at[slot], sibling).wait_recv()
        total = total + recv_d[slot].astype(F32)
    mean = total * (1.0 / NREP)
    for copy in copies_w:
        copy.wait_recv()
    parts = jnp.dot(jnp.concatenate(split3(mean), 0), wfull[...], preferred_element_type=F32)
    left = parts[0:CH] + parts[CH : 2 * CH] + parts[2 * CH :]

    for h in range(RANK // 128):
        product = outer_rows(left[:, 128 * h : 128 * h + 128], mean)
        for u in range(128 // UNIT):
            for r in range(NREP):
                i, j = UNIT * u + 8 * (r // 4), 128 * (r % 4)
                mpart[h * (128 // UNIT) + u, r] = product[i : i + 8, j : j + 128]
    lrow[...] = left
    leftbuf[mine, :] = left
    units = [pl.ds(start // UNIT, (stop - start) // UNIT) for start, stop in PIECES]
    copies_m = []
    for p, unit in enumerate(units):
        copies_m.append(
            [
                push(mpart.at[unit, chunk], recv_m.at[k, unit], sem_m.at[p, k], to)
                for k, (to, chunk) in enumerate(planes[p])
            ]
        )
    copies_lz = [push(lrow, leftbuf.at[mine], sem_lz.at[k], to) for k, to in enumerate(along_z)]

    copies_y, copies_f = [], []
    copies_lx = None
    for event in SCHEDULE:
        if event == "m":
            p = len(copies_y)
            for copy in copies_m[p]:
                copy.wait_recv()
            total = mpart[units[p], owned[p]]
            for k in range(len(replicas)):
                total = total + recv_m[k, units[p]]
            mrow[units[p]] = total
            copies_y.append(
                [push(mrow.at[units[p]], recv_y.at[k, units[p]], sem_y.at[p, k], to) for k, to in enumerate(lines[p])]
            )
        elif event == "l":
            for copy in copies_lz:
                copy.wait_recv()
            src = leftbuf.at[pl.ds(x * NZ * CH, NZ * CH)]
            copies_lx = [push(src, src, sem_lx.at[k], to) for k, to in enumerate(along_x)]
        else:
            p = len(copies_f)
            for copy in copies_y[p]:
                copy.wait_recv()
            total = mrow[units[p]]
            for k in range(NY - 1):
                total = total + recv_y[k, units[p]]
            mfull[units[p], owned[p]] = total
            src = mfull.at[units[p], owned[p]]
            copies_f.append([push(src, src, sem_f.at[p, k], to) for k, (to, _) in enumerate(planes[p])])
    waited = len(sends) - 2 * len(replicas)
    for copy in sends[:waited]:
        copy.wait_send()
    for copy in copies_lx:
        copy.wait_recv()
    for g in range(4):
        left_t[:, 128 * g : 128 * g + 128] = jnp.transpose(leftbuf[128 * g : 128 * g + 128, :])

    rank = jnp.where(c == 0, ranks_ref[0], ranks_ref[1])
    pairs = []
    for p, (start, stop) in enumerate(PIECES):
        n = stop - start
        block = start // 128 * 128
        less = None
        if p > 0:
            parts = [solved[i, 0:start, :] for i in range(3)]
            above = split3(a_ref[0:start, block : block + 128])
            above = jnp.concatenate([above[0], above[0], above[1], above[0], above[2], above[1]], 0)
            less = lax.dot_general(
                above, six_rows(parts), (((0,), (0,)), ((), ())), preferred_element_type=F32
            )[start - block : stop - block, :]
        for copy in copies_f[p]:
            copy.wait_recv()
        rows = []
        for u in range(start // UNIT, stop // UNIT):
            for g in range(8):
                rows.append(jnp.concatenate([mfull[u, 4 * g + t] for t in range(4)], 1))
        wide = jnp.concatenate(rows, 0)
        if p > 0:
            wide = wide - less[:, 0:COLS]
        parts = split3(wide)
        three = jnp.dot(jnp.concatenate(parts, 0), wfull[...], preferred_element_type=F32)
        row = lax.broadcasted_iota(jnp.int32, (n, RANK), 0)
        column = lax.broadcasted_iota(jnp.int32, (n, RANK), 1)
        filler = jnp.where((row + start == column) & (column >= rank), 1.0, 0.0)
        a_ref[start:stop, 0:RANK] = three[0:n] + three[n : 2 * n] + three[2 * n :] + filler
        a_ref[start:stop, RANK:] = jnp.where(row == column, 1.0, 0.0).astype(F32)[:, 0:128]
        eliminate_rows(a_ref, start, stop)
        inverse = six_lanes(a_ref[start:stop, RANK : RANK + n])
        mine = pl.ds(start, n)

        rows = jnp.dot(inverse, six_rows(parts), preferred_element_type=F32)
        last = stop == RANK
        factors_all[c, mine, :] = rows.astype(BF16)
        if not last:
            for i, part in enumerate(split3(rows)):
                solved[i, start:stop, 0:COLS] = part
        for t in range(4):
            blocks[t, mine, :] = rows[:, 128 * t : 128 * t + 128]
        src = factors_all.at[c, mine]
        pairs.append(push(src, src, sem_p.at[2 + 3 * p], sibling))
        pairs.append(push(blocks.at[y // 2, mine], piece_all.at[c, mine], sem_p.at[4 + 3 * p], sibling))
        piece_all[c, mine, :] = blocks[y // 2, mine, :]

        wide = left_t[start:stop, :]
        if p > 0:
            wide = wide - less[:, COLS:]
        rows = jnp.dot(inverse, six_rows(split3(wide)), preferred_element_type=F32)
        if not last:
            for i, part in enumerate(split3(rows)):
                solved[i, start:stop, COLS:] = part
        low_rows, high_rows = rows[:, 0:ROWS].astype(BF16), rows[:, ROWS:].astype(BF16)
        own_side = jnp.broadcast_to(c, (n, ROWS)) == 0
        obuf[mine, :] = jnp.where(own_side, high_rows, low_rows)
        pairs.append(push(obuf.at[mine], orth_all.at[c, mine], sem_p.at[3 + 3 * p], sibling))
        orth_all[c, mine, :] = jnp.where(own_side, low_rows, high_rows)
    for copy in pairs:
        copy.wait_recv()
    for copy in sends[waited:]:
        copy.wait_send()


def factor_all(ranks, deltas, warm):
    others, pieces = len(REP_STEPS), len(PIECES)
    total = 2 + others + (NY - 1) + pieces * (2 * others + NY - 1 + 3) + (NZ - 1) + (NX - 1)
    dma = pltpu.SemaphoreType.DMA
    return pl.pallas_call(
        factor_kernel,
        out_shape=(
            jax.ShapeDtypeStruct((2, RANK, ROWS), BF16),
            jax.ShapeDtypeStruct((2, RANK, COLS), BF16),
            jax.ShapeDtypeStruct((2, RANK, 128), F32),
        ),
        in_specs=[IN_HBM] * 3,
        out_specs=(VMEM,) * 3,
        scratch_shapes=[
            pltpu.SMEM((2,), jnp.int32),
            pltpu.VMEM((32, 2, RANK), F32),
            pltpu.VMEM((2 * ROWS, COLS), BF16),
            pltpu.VMEM((NREP, CH, COLS), BF16),
            pltpu.VMEM((2, 32, RANK), BF16),
            pltpu.VMEM((COLS, RANK), BF16),
            pltpu.VMEM((UNITS, NREP, 8, 128), F32),
            pltpu.VMEM((others, UNITS, 8, 128), F32),
            pltpu.VMEM((NY - 1, UNITS, 8, 128), F32),
            pltpu.VMEM((UNITS, 8, 128), F32),
            pltpu.VMEM((UNITS, NREP, 8, 128), F32),
            pltpu.VMEM((CH, RANK), F32),
            pltpu.VMEM((2 * ROWS, RANK), F32),
            pltpu.VMEM((RANK, 2 * ROWS), F32),
            pltpu.VMEM((RANK, RANK + 128), F32),
            pltpu.VMEM((3, RANK, WIDE), BF16),
            pltpu.VMEM((RANK, ROWS), BF16),
            pltpu.VMEM((4, RANK, 128), F32),
            dma((3,)), dma((total,)), dma((NREP,)), dma((pieces, others)), dma((pieces, NY - 1)),
            dma((pieces, others)), dma((NZ - 1,)), dma((NX - 1,)), dma((NY - 1,)), dma((2 + 3 * pieces,)),
        ],
        compiler_params=pltpu.CompilerParams(
            collective_id=1, has_side_effects=True, vmem_limit_bytes=32 * 2**20
        ),
        name="factor_all",
        cost_estimate=pl.CostEstimate(flops=10**9, bytes_accessed=0, transcendentals=0),
    )(*(pltpu.with_memory_space_constraint(a, pltpu.HBM) for a in (ranks, deltas, warm)))


def update_kernel(orth, factors, piece, weights, momentum, new_weights, new_momentum, new_factors, turned):
    offset = lax.axis_index("fsdp") % 4 * 32
    for m in range(2):
        approx = lax.dot_general(orth[m], factors[m], (((0,), (0,)), ((), ())), preferred_element_type=F32)
        fresh = OUTER_MOMENTUM * momentum[m] + approx
        new_momentum[m] = fresh
        new_weights[m] = weights[m] - OUTER_RATE * (approx + OUTER_MOMENTUM * fresh)
        turned[m] = jnp.transpose(piece[m])
        new_factors[:, m, :] = turned[m, pl.ds(offset, 32), :]


def update(orth, factors, piece, weights, momentum):
    return pl.pallas_call(
        update_kernel,
        out_shape=(
            jax.ShapeDtypeStruct((2, ROWS, COLS), F32),
            jax.ShapeDtypeStruct((2, ROWS, COLS), F32),
            jax.ShapeDtypeStruct((32, 2, RANK), F32),
        ),
        in_specs=[VMEM] * 5,
        out_specs=(VMEM,) * 3,
        scratch_shapes=[pltpu.VMEM((2, 128, RANK), F32)],
        compiler_params=pltpu.CompilerParams(vmem_limit_bytes=32 * 2**20),
        name="update",
    )(orth, factors, piece, weights, momentum)


def shards(deltas, weights, momentum, warm_factors, matrix_ranks):
    orth, factors, piece = factor_all(matrix_ranks, deltas, warm_factors)
    return update(orth, factors, piece, weights, momentum)


def solution(mesh):
    placed = (
        P("rep", None, "fsdp", None),
        P(None, "fsdp", None),
        P(None, "fsdp", None),
        P("fsdp", None, None),
        P(),
    )
    return jax.shard_map(
        shards,
        mesh=mesh,
        in_specs=placed,
        out_specs=(P(None, "fsdp", None), P(None, "fsdp", None), P("fsdp", None, None)),
        check_vma=False,
    )
```

```python
import jax
import jax.numpy as jnp
from jax import lax
from jax.experimental import pallas as pl
from jax.experimental.pallas import tpu as pltpu
from jax.sharding import PartitionSpec as P

OUTER_RATE = 0.7
OUTER_MOMENTUM = 0.9
MESH = pl.DeviceIdType.MESH
F32 = jnp.float32
BF16 = jnp.bfloat16
NX, NZ, NY = 4, 8, 8
NREP = NX * NZ
ROWS, COLS, RANK = 256, 512, 256
CH = 16
UNIT = 64
UNITS = RANK // UNIT
PIECES = ((0, 128), (128, 256))
PLANES = "zy"
SCHEDULE = "mmlyy"
WIDE = COLS + 2 * ROWS
VMEM = pl.BlockSpec(memory_space=pltpu.VMEM)
IN_HBM = pl.BlockSpec(memory_space=pltpu.HBM)
PLANE_STEPS = [(dx, d) for dx in range(NX) for d in range(NY) if dx and d]
REP_STEPS = [(dx, dz) for dx in range(NX) for dz in range(NZ) if (dx, dz) != (0, 0)]


def position():
    rep, fsdp = lax.axis_index("rep"), lax.axis_index("fsdp")
    return rep // NZ, rep % NZ, fsdp // 2, fsdp % 2


def split3(x):
    high = x.astype(BF16)
    rest = x - high.astype(F32)
    mid = rest.astype(BF16)
    low = (rest - mid.astype(F32)).astype(BF16)
    return high, mid, low


def outer_rows(a, b):
    ah, am, al = split3(a)
    bh, bm, bl = split3(b)
    left = jnp.concatenate([ah, ah, am, ah, al, am], 0)
    right = jnp.concatenate([bh, bm, bh, bl, bh, bm], 0)
    return lax.dot_general(left, right, (((0,), (0,)), ((), ())), preferred_element_type=F32)


def six_lanes(a):
    high, mid, low = split3(a)
    return jnp.concatenate([high, high, mid, high, low, mid], 1)


def six_rows(parts):
    high, mid, low = parts
    return jnp.concatenate([high, mid, high, low, high, mid], 0)


def spread(x):
    return jnp.broadcast_to(x, (8, 128))


def eliminate(tiles, lane0, groups, width):
    sub = lax.broadcasted_iota(jnp.int32, (8, 128), 0)
    pivots = [None] * groups
    for b in range(groups * 8 // width):
        first = b * width // 8
        col = []
        for k in range(width):
            at = lane0 + b * width + k
            col.append([None] * first + [spread(tiles[0][g][:, at : at + 1]) for g in range(first, groups)])
        for j in range(width):
            g0, s = divmod(b * width + j, 8)
            pivot = spread(col[j][g0][s : s + 1, :])
            inverse = 1.0 / pivot
            factor = [None] * groups
            for g in range(g0, groups):
                factor[g] = jnp.where(sub > s, col[j][g], 0.0) if g == g0 else col[j][g]
            for k in range(j + 1, width):
                row = spread(col[k][g0][s : s + 1, :]) * inverse
                for g in range(g0, groups):
                    col[k][g] = col[k][g] - factor[g] * row
            for t in tiles:
                row = spread(t[g0][s : s + 1, :]) * inverse
                for g in range(g0, groups):
                    t[g] = t[g] - factor[g] * row
            pivots[g0] = pivot if s == 0 else jnp.where(sub == s, pivot, pivots[g0])
    for g in range(groups):
        scale = lax.rsqrt(pivots[g])
        for t in tiles:
            t[g] = t[g] * scale


def eliminate_rows(a_ref, start, stop):
    width = 32
    groups = width // 8
    for k0 in range(start, stop, width):
        t0 = k0 // 128
        cols = list(range(t0, RANK // 128)) + [RANK // 128]
        rows = [slice(k0 + 8 * g, k0 + 8 * g + 8) for g in range(groups)]
        tiles = [[a_ref[r, 128 * t : 128 * t + 128] for r in rows] for t in cols]
        eliminate(tiles, k0 % 128, groups, 16)
        for i, t in enumerate(cols):
            for g, r in enumerate(rows):
                a_ref[r, 128 * t : 128 * t + 128] = tiles[i][g]
        if k0 + width < stop:
            block = slice(128 * t0, 128 * t0 + 128)
            update = outer_rows(a_ref[k0 : k0 + width, block], a_ref[k0 : k0 + width, 128 * t0 :])
            rest = slice(k0 + width - 128 * t0, stop - 128 * t0)
            a_ref[k0 + width : stop, 128 * t0 :] = a_ref[k0 + width : stop, 128 * t0 :] - update[rest, :]


def factor_kernel(
    ranks_hbm, deltas_hbm, warm_hbm,
    orth_all, factors_all, piece_all,
    ranks_ref, warm_ref, dbuf, recv_d, wtmp, wfull, mpart, recv_m, recv_y, mrow, mfull, lrow, leftbuf, left_t, a_ref,
    solved, obuf, blocks, local, send, sem_d, sem_m, sem_y, sem_f, sem_lz, sem_lx, sem_w, sem_p,
):
    x, z, y, c = position()
    rep = x * NZ + z
    other = 1 - c
    here = y * 2 + c
    there = y * 2 + other

    def at(dx, dz):
        return lax.rem(x + dx, NX) * NZ + lax.rem(z + dz, NZ)

    sibling = (rep, there)
    columns = [(rep, lax.rem(y + d, NY) * 2 + c) for d in range(1, NY)]
    along_z = [(at(0, dz), here) for dz in range(1, NZ)]
    along_x = [(at(dx, 0), here) for dx in range(1, NX)]
    replicas = [(at(dx, dz), here) for dx, dz in REP_STEPS]

    def across(dx, dy):
        return lax.rem(x + dx, NX), lax.rem(y + dy, NY)

    in_xy = [across(dx, dy) for dx, dy in REP_STEPS]
    in_xy = [((to_x * NZ + z, to_y * 2 + c), to_x * NY + to_y) for to_x, to_y in in_xy]
    in_xz = [(device, device[0]) for device in replicas]
    planes = [in_xz if plane == "z" else in_xy for plane in PLANES]
    owned = [rep if plane == "z" else x * NY + y for plane in PLANES]
    lines = [columns if plane == "z" else along_z for plane in PLANES]
    corners = [in_xy[k][0] for k, step in enumerate(REP_STEPS) if step in PLANE_STEPS]

    local_copies = [
        pltpu.make_async_copy(ranks_hbm, ranks_ref, local.at[0]),
        pltpu.make_async_copy(warm_hbm, warm_ref, local.at[1]),
        pltpu.make_async_copy(deltas_hbm.at[0, c], dbuf.at[pl.ds(c * ROWS, ROWS)], local.at[2]),
    ]
    for copy in local_copies:
        copy.start()
    barrier = pltpu.get_barrier_semaphore()
    for device in replicas + columns + corners + [sibling]:
        pl.semaphore_signal(barrier, inc=1, device_id=device, device_id_type=MESH)

    sends = []

    def remote(src, dst, sem, device):
        return pltpu.make_async_remote_copy(
            src_ref=src, dst_ref=dst, send_sem=send.at[len(sends)], recv_sem=sem,
            device_id=device, device_id_type=MESH,
        )

    def push(src, dst, sem, device):
        copy = remote(src, dst, sem, device)
        copy.start()
        sends.append(copy)
        return copy

    for copy in local_copies:
        copy.wait()
    lane = lax.broadcasted_iota(jnp.int32, (32, RANK), 1)
    for m in range(2):
        mask = jnp.where(lane < ranks_ref[m], 1.0, 0.0).astype(BF16)
        wtmp[m] = warm_ref[:, m, :].astype(BF16) * mask
    wfull[pl.ds(here * 32, 32), :] = wtmp[c]
    pl.semaphore_wait(barrier, len(replicas) + len(columns) + len(corners) + 1)

    pair_d = push(deltas_hbm.at[0, other], dbuf.at[pl.ds(c * ROWS, ROWS)], sem_p.at[0], sibling)
    pair_w = push(wtmp.at[other], wfull.at[pl.ds(here * 32, 32)], sem_p.at[1], sibling)

    def push_d(x_to, dz):
        to = x_to * NZ + lax.rem(z + dz, NZ)
        slot = lax.rem(x_to - x + NX, NX) * NZ + dz
        push(dbuf.at[pl.ds(to * CH, CH)], recv_d.at[slot], sem_d.at[slot], (to, here))

    for dz in range(1, NZ):
        for step in range(2):
            push_d(2 * c + step, dz)
    pair_w.wait_recv()
    mine = pl.ds(y * 64, 64)
    copies_w = [push(wfull.at[mine], wfull.at[mine], sem_w.at[k], to) for k, to in enumerate(columns)]
    pair_d.wait_recv()
    for dz in range(1, NZ):
        for step in range(2):
            push_d(2 * other + step, dz)
    for dx in range(1, NX):
        push_d(lax.rem(x + dx, NX), 0)

    mine = pl.ds(rep * CH, CH)
    total = dbuf[mine, :].astype(F32)
    for dx, dz in REP_STEPS:
        slot = dx * NZ + dz
        remote(recv_d.at[slot], recv_d.at[slot], sem_d.at[slot], sibling).wait_recv()
        total = total + recv_d[slot].astype(F32)
    mean = total * (1.0 / NREP)
    for copy in copies_w:
        copy.wait_recv()
    parts = jnp.dot(jnp.concatenate(split3(mean), 0), wfull[...], preferred_element_type=F32)
    left = parts[0:CH] + parts[CH : 2 * CH] + parts[2 * CH :]

    for h in range(RANK // 128):
        product = outer_rows(left[:, 128 * h : 128 * h + 128], mean)
        for u in range(128 // UNIT):
            for r in range(NREP):
                i, j = UNIT * u + 8 * (r // 4), 128 * (r % 4)
                mpart[h * (128 // UNIT) + u, r] = product[i : i + 8, j : j + 128]
    lrow[...] = left
    leftbuf[mine, :] = left
    units = [pl.ds(start // UNIT, (stop - start) // UNIT) for start, stop in PIECES]
    copies_m = []
    for p, unit in enumerate(units):
        copies_m.append(
            [
                push(mpart.at[unit, chunk], recv_m.at[k, unit], sem_m.at[p, k], to)
                for k, (to, chunk) in enumerate(planes[p])
            ]
        )
    copies_lz = [push(lrow, leftbuf.at[mine], sem_lz.at[k], to) for k, to in enumerate(along_z)]

    copies_y, copies_f = [], []
    copies_lx = None
    for event in SCHEDULE:
        if event == "m":
            p = len(copies_y)
            for copy in copies_m[p]:
                copy.wait_recv()
            total = mpart[units[p], owned[p]]
            for k in range(len(replicas)):
                total = total + recv_m[k, units[p]]
            mrow[units[p]] = total
            copies_y.append(
                [push(mrow.at[units[p]], recv_y.at[k, units[p]], sem_y.at[p, k], to) for k, to in enumerate(lines[p])]
            )
        elif event == "l":
            for copy in copies_lz:
                copy.wait_recv()
            src = leftbuf.at[pl.ds(x * NZ * CH, NZ * CH)]
            copies_lx = [push(src, src, sem_lx.at[k], to) for k, to in enumerate(along_x)]
        else:
            p = len(copies_f)
            for copy in copies_y[p]:
                copy.wait_recv()
            total = mrow[units[p]]
            for k in range(NY - 1):
                total = total + recv_y[k, units[p]]
            mfull[units[p], owned[p]] = total
            src = mfull.at[units[p], owned[p]]
            copies_f.append([push(src, src, sem_f.at[p, k], to) for k, (to, _) in enumerate(planes[p])])
    waited = len(sends) - 2 * len(replicas)
    for copy in sends[:waited]:
        copy.wait_send()
    for copy in copies_lx:
        copy.wait_recv()
    for g in range(4):
        left_t[:, 128 * g : 128 * g + 128] = jnp.transpose(leftbuf[128 * g : 128 * g + 128, :])

    rank = jnp.where(c == 0, ranks_ref[0], ranks_ref[1])
    pairs = []
    for p, (start, stop) in enumerate(PIECES):
        n = stop - start
        block = start // 128 * 128
        less = None
        if p > 0:
            parts = [solved[i, 0:start, :] for i in range(3)]
            above = split3(a_ref[0:start, block : block + 128])
            above = jnp.concatenate([above[0], above[0], above[1], above[0], above[2], above[1]], 0)
            less = lax.dot_general(
                above, six_rows(parts), (((0,), (0,)), ((), ())), preferred_element_type=F32
            )[start - block : stop - block, :]
        left_rows = left_t[start:stop, :]
        if p > 0:
            left_rows = left_rows - less[:, COLS:]
        left_rows = six_rows(split3(left_rows))
        for copy in copies_f[p]:
            copy.wait_recv()
        rows = []
        for u in range(start // UNIT, stop // UNIT):
            for g in range(8):
                rows.append(jnp.concatenate([mfull[u, 4 * g + t] for t in range(4)], 1))
        wide = jnp.concatenate(rows, 0)
        if p > 0:
            wide = wide - less[:, 0:COLS]
        parts = split3(wide)
        three = jnp.dot(jnp.concatenate(parts, 0), wfull[...], preferred_element_type=F32)
        row = lax.broadcasted_iota(jnp.int32, (n, RANK), 0)
        column = lax.broadcasted_iota(jnp.int32, (n, RANK), 1)
        filler = jnp.where((row + start == column) & (column >= rank), 1.0, 0.0)
        a_ref[start:stop, 0:RANK] = three[0:n] + three[n : 2 * n] + three[2 * n :] + filler
        a_ref[start:stop, RANK:] = jnp.where(row == column, 1.0, 0.0).astype(F32)[:, 0:128]
        eliminate_rows(a_ref, start, stop)
        inverse = six_lanes(a_ref[start:stop, RANK : RANK + n])
        mine = pl.ds(start, n)

        rows = jnp.dot(inverse, six_rows(parts), preferred_element_type=F32)
        last = stop == RANK
        factors_all[c, mine, :] = rows.astype(BF16)
        if not last:
            for i, part in enumerate(split3(rows)):
                solved[i, start:stop, 0:COLS] = part
        for t in range(4):
            blocks[t, mine, :] = rows[:, 128 * t : 128 * t + 128]
        src = factors_all.at[c, mine]
        pairs.append(push(src, src, sem_p.at[2 + 3 * p], sibling))
        pairs.append(push(blocks.at[y // 2, mine], piece_all.at[c, mine], sem_p.at[4 + 3 * p], sibling))
        piece_all[c, mine, :] = blocks[y // 2, mine, :]

        rows = jnp.dot(inverse, left_rows, preferred_element_type=F32)
        if not last:
            for i, part in enumerate(split3(rows)):
                solved[i, start:stop, COLS:] = part
        low_rows, high_rows = rows[:, 0:ROWS].astype(BF16), rows[:, ROWS:].astype(BF16)
        own_side = jnp.broadcast_to(c, (n, ROWS)) == 0
        obuf[mine, :] = jnp.where(own_side, high_rows, low_rows)
        pairs.append(push(obuf.at[mine], orth_all.at[c, mine], sem_p.at[3 + 3 * p], sibling))
        orth_all[c, mine, :] = jnp.where(own_side, low_rows, high_rows)
    for copy in pairs:
        copy.wait_recv()
    for copy in sends[waited:]:
        copy.wait_send()


def factor_all(ranks, deltas, warm):
    others, pieces = len(REP_STEPS), len(PIECES)
    total = 2 + others + (NY - 1) + pieces * (2 * others + NY - 1 + 3) + (NZ - 1) + (NX - 1)
    dma = pltpu.SemaphoreType.DMA
    return pl.pallas_call(
        factor_kernel,
        out_shape=(
            jax.ShapeDtypeStruct((2, RANK, ROWS), BF16),
            jax.ShapeDtypeStruct((2, RANK, COLS), BF16),
            jax.ShapeDtypeStruct((2, RANK, 128), F32),
        ),
        in_specs=[IN_HBM] * 3,
        out_specs=(VMEM,) * 3,
        scratch_shapes=[
            pltpu.SMEM((2,), jnp.int32),
            pltpu.VMEM((32, 2, RANK), F32),
            pltpu.VMEM((2 * ROWS, COLS), BF16),
            pltpu.VMEM((NREP, CH, COLS), BF16),
            pltpu.VMEM((2, 32, RANK), BF16),
            pltpu.VMEM((COLS, RANK), BF16),
            pltpu.VMEM((UNITS, NREP, 8, 128), F32),
            pltpu.VMEM((others, UNITS, 8, 128), F32),
            pltpu.VMEM((NY - 1, UNITS, 8, 128), F32),
            pltpu.VMEM((UNITS, 8, 128), F32),
            pltpu.VMEM((UNITS, NREP, 8, 128), F32),
            pltpu.VMEM((CH, RANK), F32),
            pltpu.VMEM((2 * ROWS, RANK), F32),
            pltpu.VMEM((RANK, 2 * ROWS), F32),
            pltpu.VMEM((RANK, RANK + 128), F32),
            pltpu.VMEM((3, RANK, WIDE), BF16),
            pltpu.VMEM((RANK, ROWS), BF16),
            pltpu.VMEM((4, RANK, 128), F32),
            dma((3,)), dma((total,)), dma((NREP,)), dma((pieces, others)), dma((pieces, NY - 1)),
            dma((pieces, others)), dma((NZ - 1,)), dma((NX - 1,)), dma((NY - 1,)), dma((2 + 3 * pieces,)),
        ],
        compiler_params=pltpu.CompilerParams(
            collective_id=1, has_side_effects=True, vmem_limit_bytes=32 * 2**20
        ),
        name="factor_all",
        cost_estimate=pl.CostEstimate(flops=10**9, bytes_accessed=0, transcendentals=0),
    )(*(pltpu.with_memory_space_constraint(a, pltpu.HBM) for a in (ranks, deltas, warm)))


def update_kernel(orth, factors, piece, weights, momentum, new_weights, new_momentum, new_factors, turned):
    offset = lax.axis_index("fsdp") % 4 * 32
    for m in range(2):
        approx = lax.dot_general(orth[m], factors[m], (((0,), (0,)), ((), ())), preferred_element_type=F32)
        fresh = OUTER_MOMENTUM * momentum[m] + approx
        new_momentum[m] = fresh
        new_weights[m] = weights[m] - OUTER_RATE * (approx + OUTER_MOMENTUM * fresh)
        turned[m] = jnp.transpose(piece[m])
        new_factors[:, m, :] = turned[m, pl.ds(offset, 32), :]


def update(orth, factors, piece, weights, momentum):
    return pl.pallas_call(
        update_kernel,
        out_shape=(
            jax.ShapeDtypeStruct((2, ROWS, COLS), F32),
            jax.ShapeDtypeStruct((2, ROWS, COLS), F32),
            jax.ShapeDtypeStruct((32, 2, RANK), F32),
        ),
        in_specs=[VMEM] * 5,
        out_specs=(VMEM,) * 3,
        scratch_shapes=[pltpu.VMEM((2, 128, RANK), F32)],
        compiler_params=pltpu.CompilerParams(vmem_limit_bytes=32 * 2**20),
        name="update",
    )(orth, factors, piece, weights, momentum)


def shards(deltas, weights, momentum, warm_factors, matrix_ranks):
    orth, factors, piece = factor_all(matrix_ranks, deltas, warm_factors)
    return update(orth, factors, piece, weights, momentum)


def solution(mesh):
    placed = (
        P("rep", None, "fsdp", None),
        P(None, "fsdp", None),
        P(None, "fsdp", None),
        P("fsdp", None, None),
        P(),
    )
    return jax.shard_map(
        shards,
        mesh=mesh,
        in_specs=placed,
        out_specs=(P(None, "fsdp", None), P(None, "fsdp", None), P("fsdp", None, None)),
        check_vma=False,
    )
```
